256 devices in a mesh: section: 16 (over x_lo, z), tp: 16 (over x_hi, y, core).
Axes of the slice: x: 4 (x_hi: 2, x_lo: 2; x = x_hi * 2 + x_lo), y: 4, z: 8, core: 2. Of those that a mesh axis runs over, the one named last changes fastest.
Arguments:
- hidden: bfloat16 [16384, 8192], P(('section', 'tp')), may hold values from -6 to 6
- norm_gain: float32 [16, 8192], P('section'), may hold values from 0.5 to 1.5
- query_weight: bfloat16 [16, 8192, 4096], P('section', None, 'tp'), may hold values from -0.0625 to 0.0625
- kv_weight: bfloat16 [16, 8192, 1024], P('section', None, 'tp'), may hold values from -0.13368738 to 0.13368738
- out_weight: bfloat16 [16, 4096, 8192], P('section', 'tp'), may hold values from -0.09375 to 0.09375
- prompt_cache: bfloat16 [16, 4, 1024, 1024], P('section', None, 'tp'), may hold values from -320 to 320
- resp_len: int32 [128], P('section'), may hold values from 1 to 128, as said below
- prompt_id: int32 [128], P('section'), may hold values from 0 to 3
Outputs:
- next_hidden: bfloat16 [16384, 8192], P(('section', 'tp'))
The draws below stay inside these ranges and needn't reach their ends.
Inputs may be any that keep to these rules, and one draw needn't show every extreme that they name: `resp_len`: some response of the draw has exactly 128 live tokens.
All inputs are finite; a program needn't handle non-finite values.
Results may differ from the reference program's by a relative error of at most 0.011.
Values may be sent and summed in bfloat16 or wider, within the bound.
No kernel may reach another device: no remote copies, remote signals or barrier semaphores. Data moves between devices by JAX's collectives and lax.ppermute only.
A program may use at most 128 MiB of HBM per device.

```python
import math
import jax
import jax.numpy as jnp
from jax import lax

D = 8192
QH = 32
KVH = 4
HD = 128
PROMPT = 1024
NPROMPT = 4
RESP = 128
TOK_DEV = 64
SEQS = 8
TOKENS = 16384
N_SECTION = 16
N_TP = 16


def draw_resp_len(key, part):
    key = jax.random.fold_in(key, 1)
    key_len, key_pick = jax.random.split(key)
    number = N_SECTION * SEQS
    lengths = jax.random.randint(key_len, (number,), 1, RESP + 1)
    longest = jax.random.randint(key_pick, (), 0, number)
    return jnp.where(jnp.arange(number) == longest, RESP, lengths).astype(jnp.int32)


def draw_prompt_cache(key, part):
    key = jax.random.fold_in(key, 2)
    key_keys, key_vals, key_scale = jax.random.split(key, 3)
    shape_half = (N_SECTION, NPROMPT, PROMPT, KVH, HD)
    token_shape = (N_SECTION, NPROMPT, PROMPT, KVH, 1)
    scales = jnp.exp(jax.random.uniform(key_scale, token_shape, jnp.float32, math.log(0.5), math.log(3.0)))
    all_keys = jnp.clip(jax.random.normal(key_keys, shape_half, jnp.float32), -6.0, 6.0) * scales
    values = jnp.clip(jax.random.normal(key_vals, shape_half, jnp.float32), -4.0, 4.0)
    flat_shape = (N_SECTION, NPROMPT, PROMPT, KVH * HD)
    return jnp.concatenate([all_keys.reshape(flat_shape), values.reshape(flat_shape)], axis=-1).astype(jnp.bfloat16)


def draw_kv_weight(key, part):
    key = jax.random.fold_in(key, 3)
    shape_full = (N_SECTION, D, 2 * KVH * HD)
    column_scale = jnp.where(jnp.arange(2 * KVH * HD) < KVH * HD, 3.0, 1.5) * D ** (-0.5)
    entries = jnp.clip(jax.random.normal(key, shape_full, jnp.float32), -4.0, 4.0)
    return (entries * column_scale).astype(jnp.bfloat16)


def plant(drawn, key, low, high):
    spot = [jax.random.randint(jax.random.fold_in(key, axis), (), 0, length) for axis, length in enumerate(drawn.shape)]
    widest = drawn.shape.index(max(drawn.shape))
    neighbour = spot[:widest] + [(spot[widest] + 1) % drawn.shape[widest]] + spot[widest + 1:]
    return drawn.at[tuple(spot)].set(low).at[tuple(neighbour)].set(high)


def block_levels(rng, shape, cuts, smallest, top_value):
    def one(dim, blocks):
        heights = jax.random.uniform(jax.random.fold_in(jax.random.fold_in(rng, 6), dim), (blocks,), jnp.float32, smallest / len(cuts), top_value / len(cuts))
        return jnp.repeat(jnp.exp(heights), shape[dim] // blocks).reshape((-1,) + (1,) * (len(shape) - dim - 1))

    loudness = one(*cuts[0])
    for cut in cuts[1:]:
        loudness = loudness * one(*cut)
    return loudness


def gaussian(rng, dims, scale, limit, cuts=(), kind=jnp.bfloat16):
    loudness = block_levels(rng, dims, cuts, -0.22, 0.18) if cuts else 1.0
    drawn = jax.random.normal(rng, dims, jnp.float32) * scale * loudness
    return jnp.minimum(jnp.maximum(drawn, -limit), limit).astype(kind)


def setup_inputs(seed: int = 0) -> dict:
    streams_of = jax.random.split(jax.random.key(seed), 9)
    hidden = gaussian(streams_of[0], (TOKENS, D), 1.0, 6.0, ((0, 256),))
    norm_gain = jnp.clip(1.0 + 0.1 * jax.random.normal(streams_of[1], (N_SECTION, D), jnp.float32), 0.5, 1.5)
    query_weight = gaussian(streams_of[2], (N_SECTION, D, QH * HD), D ** -0.5, 0.0625, ((0, 16), (2, 16)))
    kv_weight = draw_kv_weight(jax.random.fold_in(streams_of[8], 71), 0)
    out_weight = gaussian(streams_of[4], (N_SECTION, QH * HD, D), (QH * HD) ** -0.5, 0.09375, ((0, 16), (1, 16)))
    prompt_cache = draw_prompt_cache(jax.random.fold_in(streams_of[8], 71), 0)
    resp_len = draw_resp_len(jax.random.fold_in(streams_of[8], 71), 0)
    prompt_id = plant(jax.random.randint(streams_of[7], (N_SECTION * SEQS,), 0, NPROMPT), jax.random.fold_in(streams_of[7], 1), 0, NPROMPT - 1).astype(jnp.int32)
    return {"hidden": hidden, "norm_gain": norm_gain, "query_weight": query_weight, "kv_weight": kv_weight, "out_weight": out_weight, "prompt_cache": prompt_cache, "resp_len": resp_len, "prompt_id": prompt_id}


def rope_tables(offset, length, head_width):
    half_width = head_width // 2
    position = (offset + jnp.arange(length)).astype(jnp.float32)
    inverse = jnp.exp(-(2.0 * jnp.arange(half_width).astype(jnp.float32) / head_width) * jnp.log(10000.0))
    angles = position[:, None] * inverse[None, :]
    return (jnp.cos(angles), jnp.sin(angles))

def rotate(tensor, cosine_table, sine_table):
    half_width = tensor.shape[-1] // 2
    first_half = tensor[..., :half_width]
    second_half = tensor[..., half_width:]
    return jnp.concatenate([first_half * cosine_table - second_half * sine_table, second_half * cosine_table + first_half * sine_table], axis=-1)

def one_section(section_inputs):
    hidden, norm_gain, query_weight, kv_weight, out_weight, prompt_cache, lengths, prompts = section_inputs
    row_count = hidden.shape[0]
    seq_count = lengths.shape[0]
    group_size = QH // KVH
    widened = hidden.astype(jnp.float32)
    normed = (widened * lax.rsqrt(lax.optimization_barrier(jnp.mean(widened * widened, axis=-1, keepdims=True)) + 1e-06) * norm_gain).astype(jnp.bfloat16)
    cosine_table, sine_table = rope_tables(PROMPT, RESP, HD)
    queries = jnp.dot(normed, query_weight, preferred_element_type=jnp.float32)
    queries = queries.reshape(seq_count, RESP, QH, HD).transpose(0, 2, 1, 3)
    queries = rotate(queries, cosine_table, sine_table).astype(jnp.bfloat16)
    pairs = jnp.dot(normed, kv_weight, preferred_element_type=jnp.float32).astype(jnp.bfloat16)
    pairs = pairs.reshape(seq_count, RESP, 2, KVH, HD)
    own_keys = rotate(pairs[:, :, 0].transpose(0, 2, 1, 3).astype(jnp.float32), cosine_table, sine_table).astype(jnp.bfloat16)
    own_values = pairs[:, :, 1].transpose(0, 2, 1, 3)
    chosen = jnp.take(prompt_cache, prompts, axis=0).reshape(seq_count, PROMPT, 2, KVH, HD)
    all_keys = jnp.concatenate([chosen[:, :, 0].transpose(0, 2, 1, 3), own_keys], axis=2)
    values = jnp.concatenate([chosen[:, :, 1].transpose(0, 2, 1, 3), own_values], axis=2)
    grouped = queries.reshape(seq_count, KVH, group_size, RESP, HD)
    scores = jnp.einsum('sgrqd,sgkd->sgrqk', grouped.astype(jnp.float32), all_keys.astype(jnp.float32)) * HD ** (-0.5)
    key_pos = jnp.arange(PROMPT + RESP) - PROMPT
    query_pos = jnp.arange(RESP)
    visible = (key_pos[None, None, :] < 0) | (key_pos[None, None, :] <= query_pos[None, :, None]) & (key_pos[None, None, :] < lengths[:, None, None])
    scores = jnp.where(visible[:, None, None], scores, -jnp.inf)
    maxima = lax.optimization_barrier(jnp.max(scores, axis=-1, keepdims=True))
    probs = jnp.exp(scores - maxima)
    totals = lax.optimization_barrier(jnp.sum(probs, axis=-1, keepdims=True))
    weights = lax.optimization_barrier(probs.astype(jnp.bfloat16))
    blended = jnp.einsum('sgrqk,sgkd->sgrqd', weights.astype(jnp.float32), values.astype(jnp.float32)) / totals
    live_rows = query_pos[None, :] < lengths[:, None]
    blended = jnp.where(live_rows[:, None, None, :, None], blended, 0.0)
    attended = blended.reshape(seq_count, QH, RESP, HD).transpose(0, 2, 1, 3).reshape(row_count, QH * HD).astype(jnp.bfloat16)
    group_cols = QH * HD // N_TP
    group_parts = attended.reshape(row_count, N_TP, group_cols).transpose(1, 0, 2)
    group_weights = out_weight.reshape(N_TP, group_cols, D)

    def add_group(running, pair_item):
        group_part, group_weight = pair_item
        group_term = jnp.dot(group_part, group_weight, preferred_element_type=jnp.float32).astype(jnp.bfloat16)
        group_term = lax.optimization_barrier(group_term)
        return (running + group_term.astype(jnp.float32), None)
    summed, unused = lax.scan(add_group, jnp.zeros((row_count, D), jnp.float32), (group_parts, group_weights))
    return (widened + summed).astype(jnp.bfloat16)

def reference(hidden, norm_gain, query_weight, kv_weight, out_weight, prompt_cache, resp_len, prompt_id):
    row_count = TOK_DEV * N_TP
    seq_count = row_count // RESP
    layer_out = lax.map(one_section, (hidden.reshape(N_SECTION, row_count, D), norm_gain, query_weight, kv_weight, out_weight, prompt_cache, resp_len.reshape(N_SECTION, seq_count), prompt_id.reshape(N_SECTION, seq_count)))
    return jnp.roll(layer_out, 1, axis=0).reshape(N_SECTION * row_count, D)
```

```python
import functools

import jax
import jax.numpy as jnp
from jax import lax
from jax.experimental import pallas as pl
from jax.experimental.pallas import tpu as pltpu
from jax.sharding import Mesh, PartitionSpec as P

D = 8192
QH = 32
KVH = 4
HD = 128
PROMPT = 1024
NPROMPT = 4
RESP = 128
ROWS = 64
EPS = 1e-06
F32 = jnp.float32
BF16 = jnp.bfloat16
VMEM = 48 * 1024 * 1024

PLACES = ((0, 0), (1, 0), (0, 3), (0, 1), (0, 2), (1, 3), (1, 1), (1, 2))


def shift(value, axis, by):
    size = lax.axis_size(axis)
    return lax.ppermute(value, axis, [(i, (i + by) % size) for i in range(size)])


def params(**kw):
    return pltpu.CompilerParams(vmem_limit_bytes=VMEM, **kw)


def norm_kernel(x_ref, gain_ref, out_ref):
    wide = x_ref[...].astype(F32)
    mean = jnp.mean(wide * wide, axis=-1, keepdims=True)
    out_ref[...] = (wide * lax.rsqrt(mean + EPS) * gain_ref[...]).astype(BF16)


def norm(hidden, gain):
    return pl.pallas_call(
        norm_kernel,
        out_shape=jax.ShapeDtypeStruct((ROWS, D), BF16),
        grid=(2,),
        in_specs=[
            pl.BlockSpec((ROWS // 2, D), lambda i: (i, 0)),
            pl.BlockSpec((1, D), lambda i: (0, 0)),
        ],
        out_specs=pl.BlockSpec((ROWS // 2, D), lambda i: (i, 0)),
        compiler_params=params(),
        name="norm",
    )(hidden, gain)


def turned(value, cosines, sines):
    return value * cosines + pltpu.roll(value, HD // 2, 1) * sines


def query_kernel(count, *refs):
    pieces = refs[:count]
    wa_ref, wb_ref, cos_ref, sin_ref, out_ref, acc_ref = refs[count:]
    step = pl.program_id(0)
    rows = jnp.concatenate([piece[...] for piece in pieces], axis=0)
    half = wa_ref.shape[1]

    @pl.when(step == 0)
    def _():
        acc_ref[...] = jnp.zeros_like(acc_ref)

    acc_ref[:, :half] += jnp.dot(rows, wa_ref[...], preferred_element_type=F32)
    acc_ref[:, half:] += jnp.dot(rows, wb_ref[...], preferred_element_type=F32)

    @pl.when(step == pl.num_programs(0) - 1)
    def _():
        for block in range(out_ref.shape[0]):
            for head in range(4):
                part = acc_ref[block * ROWS : (block + 1) * ROWS, head * HD : (head + 1) * HD]
                out_ref[block, head * ROWS : (head + 1) * ROWS, :] = turned(
                    part, cos_ref[...], sin_ref[...]
                ).astype(BF16)


def project_queries(pieces, own, other, cosines, sines):
    depth = 4096
    rows = sum(piece.shape[0] for piece in pieces)
    half = own.shape[1]
    return pl.pallas_call(
        functools.partial(query_kernel, len(pieces)),
        out_shape=jax.ShapeDtypeStruct((rows // ROWS, 4 * ROWS, HD), BF16),
        grid=(D // depth,),
        in_specs=[pl.BlockSpec((piece.shape[0], depth), lambda k: (0, k)) for piece in pieces]
        + [pl.BlockSpec((depth, half), lambda k: (k, 0))] * 2
        + [pl.BlockSpec((ROWS, HD), lambda k: (0, 0))] * 2,
        out_specs=pl.BlockSpec((rows // ROWS, 4 * ROWS, HD), lambda k: (0, 0, 0)),
        scratch_shapes=[pltpu.VMEM((rows, 2 * half), F32)],
        compiler_params=params(),
        cost_estimate=pl.CostEstimate(
            flops=2 * rows * D * 2 * half,
            bytes_accessed=2 * D * (rows + 2 * half),
            transcendentals=0,
        ),
        name="queries",
    )(*pieces, own, other, cosines, sines)


def dot_t(a, b):
    return lax.dot_general(a, b, (((1,), (1,)), ((), ())), preferred_element_type=F32)


def pair_kernel(count, *refs):
    pieces = refs[:count]
    core_ref, wa_ref, wb_ref, cos_ref, sin_ref, out_ref, acc_ref = refs[count:]
    step = pl.program_id(0)
    rows = jnp.concatenate([piece[...] for piece in pieces], axis=0)
    weight = jnp.concatenate([wa_ref[...], wb_ref[...]], axis=0)

    @pl.when(step == 0)
    def _():
        acc_ref[...] = jnp.zeros_like(acc_ref)

    acc_ref[...] += dot_t(rows, weight)

    @pl.when(step == pl.num_programs(0) - 1)
    def _():
        pairs = acc_ref[...].astype(BF16).astype(F32)
        pairs = jnp.where(core_ref[0] == 0, pairs, pltpu.roll(pairs, HD // 2, 1))
        for block in range(out_ref.shape[0]):
            part = pairs[block * ROWS : (block + 1) * ROWS, :]
            out_ref[block] = turned(part, cos_ref[...], sin_ref[...]).astype(BF16)


def project_pairs(pieces, core, own, other, cosines, sines):
    depth = 4096
    rows = sum(piece.shape[0] for piece in pieces)
    return pl.pallas_call(
        functools.partial(pair_kernel, len(pieces)),
        out_shape=jax.ShapeDtypeStruct((rows // ROWS, ROWS, HD), BF16),
        grid=(D // depth,),
        in_specs=[pl.BlockSpec((piece.shape[0], depth), lambda k: (0, k)) for piece in pieces]
        + [pl.BlockSpec(memory_space=pltpu.SMEM)]
        + [pl.BlockSpec((HD // 2, depth), lambda k: (0, k))] * 2
        + [pl.BlockSpec((ROWS, HD), lambda k: (0, 0))] * 2,
        out_specs=pl.BlockSpec((rows // ROWS, ROWS, HD), lambda k: (0, 0, 0)),
        scratch_shapes=[pltpu.VMEM((rows, HD), F32)],
        compiler_params=params(),
        cost_estimate=pl.CostEstimate(
            flops=2 * rows * D * HD, bytes_accessed=2 * D * (rows + HD), transcendentals=0
        ),
        name="pairs",
    )(*pieces, core, own, other, cosines, sines)


def sort_kernel(key_ref, value_ref, out_ref):
    out_ref[0, :, :, :HD] = key_ref[...]
    out_ref[0, :, :, HD:] = value_ref[...]


def sort_cache(cache):
    return pl.pallas_call(
        sort_kernel,
        out_shape=jax.ShapeDtypeStruct((2 * KVH, NPROMPT, ROWS, 2 * HD), BF16),
        grid=(2 * KVH,),
        in_specs=[
            pl.BlockSpec((NPROMPT, ROWS, HD), lambda i: (0, 0, i // 2)),
            pl.BlockSpec((NPROMPT, ROWS, HD), lambda i: (0, 0, KVH + i // 2)),
        ],
        out_specs=pl.BlockSpec((1, NPROMPT, ROWS, 2 * HD), lambda i: (i, 0, 0, 0)),
        compiler_params=params(),
        name="sort_cache",
    )(cache, cache)


def prompt_kernel(prompt_ref, q_ref, own_ref, other_ref, acc_ref, state_ref):
    queries = q_ref[0]
    half = PROMPT // 2
    own = own_ref[...].reshape(half, 2 * HD)
    other = other_ref[...].reshape(half, 2 * HD)
    score_a = dot_t(queries, own[:, :HD]) * HD ** (-0.5)
    score_b = dot_t(queries, other[:, :HD]) * HD ** (-0.5)
    top = jnp.maximum(
        jnp.max(score_a, axis=-1, keepdims=True), jnp.max(score_b, axis=-1, keepdims=True)
    )
    prob_a = jnp.exp(score_a - top)
    prob_b = jnp.exp(score_b - top)
    total = jnp.sum(prob_a, axis=-1, keepdims=True) + jnp.sum(prob_b, axis=-1, keepdims=True)
    acc_ref[0] = jnp.dot(
        prob_a.astype(BF16), own[:, HD:], preferred_element_type=F32
    ) + jnp.dot(prob_b.astype(BF16), other[:, HD:], preferred_element_type=F32)
    lane = lax.broadcasted_iota(jnp.int32, (4 * ROWS, HD), 1)
    state_ref[0] = jnp.where(lane < HD // 2, top, total)


def attend_prompt(queries, own, other, prompts):
    count = queries.shape[0]
    shape = jax.ShapeDtypeStruct((count, 4 * ROWS, HD), F32)
    block = pl.BlockSpec((1, 4 * ROWS, HD), lambda i, p: (i, 0, 0))
    cache = pl.BlockSpec((8, 1, ROWS, 2 * HD), lambda i, p: (0, p[i], 0, 0))
    return pl.pallas_call(
        prompt_kernel,
        out_shape=(shape, shape),
        grid_spec=pltpu.PrefetchScalarGridSpec(
            num_scalar_prefetch=1,
            grid=(count,),
            in_specs=[block, cache, cache],
            out_specs=(block, block),
        ),
        compiler_params=params(),
        cost_estimate=pl.CostEstimate(
            flops=count * 4 * 4 * ROWS * PROMPT * HD,
            bytes_accessed=count * PROMPT * HD * 6,
            transcendentals=count * 4 * ROWS * PROMPT,
        ),
        name="attend_prompt",
    )(prompts, queries, own, other)


def own_kernel(
    info_ref, q_ref, acc_ref, state_ref, key_a, key_b, value_a, value_b, out_ref
):
    i = pl.program_id(0)
    length = info_ref[0, i]
    core = info_ref[1, i]
    queries = q_ref[0]
    keys = jnp.concatenate([key_a[0, 0], key_b[0, 0]], axis=0)
    values = jnp.concatenate([value_a[0, 0], value_b[0, 0]], axis=0)
    scores = dot_t(queries, keys) * HD ** (-0.5)
    row = lax.broadcasted_iota(jnp.int32, (4 * ROWS, HD), 0) % ROWS + core * ROWS
    lane = lax.broadcasted_iota(jnp.int32, (4 * ROWS, HD), 1)
    place = jnp.where(lane < ROWS, lane + core * ROWS, lane - core * ROWS)
    visible = (place <= row) & (place < length)
    scores = jnp.where(visible, scores, -jnp.inf)
    top_a = state_ref[0, :, :1]
    total_a = state_ref[0, :, HD // 2 : HD // 2 + 1]
    top = jnp.maximum(top_a, jnp.max(scores, axis=-1, keepdims=True))
    scale = jnp.exp(top_a - top)
    probs = jnp.exp(scores - top)
    total = total_a * scale + jnp.sum(probs, axis=-1, keepdims=True)
    blended = acc_ref[0] * scale + jnp.dot(
        probs.astype(BF16), values, preferred_element_type=F32
    )
    blended = jnp.where(row < length, blended / total, 0.0).astype(BF16)
    for head in range(4):
        out_ref[:, head * HD : (head + 1) * HD] = blended[head * ROWS : (head + 1) * ROWS, :]


def attend_own(queries, acc, state, pairs_own, pairs_other, info):
    count = queries.shape[0]
    block = pl.BlockSpec((1, 4 * ROWS, HD), lambda i, t: (i, 0, 0))
    key = pl.BlockSpec((1, 1, ROWS, HD), lambda i, t: (t[2, i], t[3, i], 0, 0))
    value = pl.BlockSpec((1, 1, ROWS, HD), lambda i, t: (1 - t[2, i], t[4, i], 0, 0))
    return pl.pallas_call(
        own_kernel,
        out_shape=jax.ShapeDtypeStruct((count * ROWS, 4 * HD), BF16),
        grid_spec=pltpu.PrefetchScalarGridSpec(
            num_scalar_prefetch=1,
            grid=(count,),
            in_specs=[block, block, block, key, key, value, value],
            out_specs=pl.BlockSpec((ROWS, 4 * HD), lambda i, t: (i, 0)),
        ),
        compiler_params=params(),
        cost_estimate=pl.CostEstimate(
            flops=count * 4 * 4 * ROWS * RESP * HD,
            bytes_accessed=count * 4 * ROWS * HD * 12,
            transcendentals=count * 4 * ROWS * RESP,
        ),
        name="attend_own",
    )(info, queries, acc, state, pairs_own, pairs_other, pairs_own, pairs_other)


def output_kernel(x_ref, wa_ref, wb_ref, *out_refs):
    half = wa_ref.shape[0]
    total = jnp.dot(x_ref[:, :half], wa_ref[...], preferred_element_type=F32)
    total += jnp.dot(x_ref[:, half:], wb_ref[...], preferred_element_type=F32)
    for block, out_ref in enumerate(out_refs):
        out_ref[...] = total[block * ROWS : (block + 1) * ROWS, :].astype(BF16)


def project_out(attended, own, other, start, width):
    count = attended.shape[0] // ROWS
    tile = 1024
    first = start // tile
    half = own.shape[0]
    return pl.pallas_call(
        output_kernel,
        out_shape=[jax.ShapeDtypeStruct((ROWS, width), BF16)] * count,
        grid=(width // tile,),
        in_specs=[
            pl.BlockSpec((count * ROWS, 2 * half), lambda n: (0, 0)),
            pl.BlockSpec((half, tile), lambda n: (0, n + first)),
            pl.BlockSpec((half, tile), lambda n: (0, n + first)),
        ],
        out_specs=[pl.BlockSpec((ROWS, tile), lambda n: (0, n))] * count,
        compiler_params=params(),
        cost_estimate=pl.CostEstimate(
            flops=2 * count * ROWS * 2 * half * width,
            bytes_accessed=2 * width * (2 * half + count * ROWS),
            transcendentals=0,
        ),
        name="project_out",
    )(attended, own, other)


def sum_kernel(*refs):
    total = refs[0][...].astype(F32)
    for ref in refs[1:-1]:
        total += ref[...].astype(F32)
    refs[-1][...] = total.astype(BF16)


def split_kernel(a_ref, b_ref, low_ref, high_ref):
    total = (a_ref[...].astype(F32) + b_ref[...].astype(F32)).astype(BF16)
    half = low_ref.shape[1]
    low_ref[...] = total[:, :half]
    high_ref[...] = total[:, half:]


def split_sum(a, b):
    half = jax.ShapeDtypeStruct((a.shape[0], a.shape[1] // 2), BF16)
    return pl.pallas_call(
        split_kernel, out_shape=(half, half), compiler_params=params(), name="split_sum"
    )(a, b)


def relay_kernel(a_ref, up_ref, b_ref, down_ref, a_out, b_out):
    half = up_ref.shape[1]
    a_out[:, :half] = (a_ref[:, :half].astype(F32) + up_ref[...].astype(F32)).astype(BF16)
    a_out[:, half:] = a_ref[:, half:]
    b_out[:, :half] = b_ref[:, :half]
    b_out[:, half:] = (b_ref[:, half:].astype(F32) + down_ref[...].astype(F32)).astype(BF16)


def relay_sum(a, up, b, down):
    whole = jax.ShapeDtypeStruct(a.shape, BF16)
    return pl.pallas_call(
        relay_kernel, out_shape=(whole, whole), compiler_params=params(), name="relay_sum"
    )(a, up, b, down)


def add(*terms):
    return pl.pallas_call(
        sum_kernel,
        out_shape=jax.ShapeDtypeStruct(terms[0].shape, BF16),
        compiler_params=params(),
        name="add",
    )(*terms)


def after(value, *others):
    return lax.optimization_barrier((value, *others))[0]


def rope_tables():
    half = HD // 2
    position = (PROMPT + jnp.arange(RESP)).astype(F32)
    inverse = jnp.exp(-(2.0 * jnp.arange(half).astype(F32) / HD) * jnp.log(10000.0))
    angles = position[:, None] * inverse[None, :]
    cosines, sines = jnp.cos(angles), jnp.sin(angles)
    return (
        jnp.concatenate([cosines, cosines], axis=1),
        jnp.concatenate([-sines, sines], axis=1),
    )


def body(hidden, norm_gain, query_weight, kv_weight, out_weight, prompt_cache, resp_len, prompt_id):
    xh, y, core = lax.axis_index("xh"), lax.axis_index("y"), lax.axis_index("c")
    wq, wkv, wo = query_weight[0], kv_weight[0].T, out_weight[0]
    chips = ("xh", "y")

    normed = norm(hidden, norm_gain)
    b10 = shift(normed, "xh", 1)
    b03 = shift(normed, "y", 1)
    b01 = shift(normed, "y", -1)
    wkv_other = shift(wkv, "c", 1)
    wq_other = shift(wq, "c", 1)
    wo_other = shift(wo, "c", 1)
    cache = sort_cache(prompt_cache[0])

    cosines, sines = rope_tables()
    cosines = lax.dynamic_slice_in_dim(cosines, core * ROWS, ROWS, 0)
    sines = lax.dynamic_slice_in_dim(sines, core * ROWS, ROWS, 0)
    key_cosines = jnp.where(xh == 0, cosines, 1.0)
    key_sines = jnp.where(xh == 0, sines, 0.0)

    def pick(values, index):
        lanes = jnp.arange(8)
        return jnp.sum(jnp.where(index[:, None] == lanes[None, :], values[None, :], 0), axis=1)

    responses = jnp.stack([(xh ^ dx) * 4 + (y + dy) % 4 for dx, dy in PLACES])
    prompts = pick(prompt_id, responses).astype(jnp.int32)
    lengths = pick(resp_len, responses)
    maker_y = xh * 2 + y // 2
    table = [0] * 8
    for at, (dx, dy) in enumerate(PLACES):
        table[dx * 4 + dy] = at
    table = jnp.array(table, jnp.int32)
    away = (responses % 4 - maker_y) % 4
    key_at = pick(table, (responses // 4) * 4 + away)
    value_at = pick(table, (1 - responses // 4) * 4 + away)
    info = jnp.stack(
        [
            lengths,
            jnp.full((8,), core, jnp.int32),
            jnp.full((8,), y % 2, jnp.int32),
            key_at,
            value_at,
        ]
    ).astype(jnp.int32)
    core_word = jnp.full((1,), core, jnp.int32)

    b03 = after(b03, wkv_other, wq_other, wo_other, cache, info, key_cosines, key_sines)
    b01 = after(b01, b03)
    top02 = shift(b03[: ROWS // 2], "y", 1)
    low02 = shift(b01[ROWS // 2 :], "y", -1)
    b13 = shift(b10, "y", 1)
    b11 = shift(b10, "y", -1)
    top12 = shift(top02, "xh", 1)
    low12 = shift(low02, "xh", 1)
    cache = lax.all_to_all(after(cache, top02, low02), chips, 0, 0, tiled=True)
    cache_other = shift(cache, "c", 1)

    near = [normed, b10, b03, b01, top02, low02]
    far = [b13, b11, top12, low12]
    pairs_near = project_pairs(near, core_word, wkv, wkv_other, key_cosines, key_sines)
    q_near = project_queries(near, wq, wq_other, cosines, sines)
    far[0] = after(far[0], pairs_near, q_near)
    pairs_far = project_pairs(far, core_word, wkv, wkv_other, key_cosines, key_sines)
    pairs = jnp.concatenate([pairs_near, pairs_far], axis=0)
    straight = [(g, 2 * g) for g in range(4)] + [(4 + g, 2 * g + 1) for g in range(4)]
    crossed = [(g, 2 * g + 1) for g in range(4)] + [(4 + g, 2 * g) for g in range(4)]
    pairs = jnp.stack(
        [lax.ppermute(pairs, chips, straight), lax.ppermute(pairs, chips, crossed)]
    )
    pairs_other = shift(pairs, "c", 1)
    q_far = project_queries(far, wq, wq_other, cosines, sines)
    acc, state = attend_prompt(q_far, cache, cache_other, prompts[5:])
    acc_near, state_near = attend_prompt(q_near, cache, cache_other, after(prompts[:5], acc))
    pairs = after(pairs, acc_near)
    att_far = attend_own(q_far, acc, state, pairs, pairs_other, info[:, 5:])

    parts = 2
    width = D // parts
    far = []
    sent = []
    for part in range(parts):
        p13, p11, p12 = project_out(att_far, wo, wo_other, part * width, width)
        sent.append((shift(p11, "y", 1), shift(p13, "y", -1), shift(p12, "xh", 1)))
        att_far = after(att_far, p11)
    att_near = attend_own(
        q_near, acc_near, state_near, after(pairs, p11), pairs_other, info[:, :5]
    )
    mine = []
    for part in range(parts):
        mine.append(project_out(att_near, wo, wo_other, part * width, width))
        att_near = after(att_near, mine[-1][0])
    hops = []
    for part in range(parts):
        p00, p10, p03, p01, p02 = mine[part]
        up, down = split_sum(p02, sent[part][2])
        hops.append((shift(up, "y", 1), shift(down, "y", -1)))
    lasts = []
    for part in range(parts):
        p00, p10, p03, p01, p02 = mine[part]
        across = shift(add(p10, sent[part][0], sent[part][1]), "xh", 1)
        p01, p03 = relay_sum(p01, hops[part][0], p03, hops[part][1])
        lasts.append((shift(p01, "y", 1), shift(p03, "y", -1), across))
    outs = []
    for part in range(parts):
        own_rows = hidden[:, part * width : (part + 1) * width]
        total = add(own_rows, mine[part][0], *lasts[part])
        outs.append(
            lax.ppermute(total, ("xl", "z"), [(i, (i + 1) % 16) for i in range(16)])
        )
    return jnp.concatenate(outs, axis=1)


def solution(mesh):
    whole = Mesh(mesh.devices.reshape(2, 8, 2, 4, 2), ("xl", "z", "xh", "y", "c"))
    section, tp = ("xl", "z"), ("xh", "y", "c")
    in_specs = (
        P(section + tp, None),
        P(section, None),
        P(section, None, tp),
        P(section, None, tp),
        P(section, tp, None),
        P(section, None, tp, None),
        P(section),
        P(section),
    )
    out_specs = P(section + tp, None)
    return jax.shard_map(body, mesh=whole, in_specs=in_specs, out_specs=out_specs, check_vma=False)
```

```python
import functools

import jax
import jax.numpy as jnp
from jax import lax
from jax.experimental import pallas as pl
from jax.experimental.pallas import tpu as pltpu
from jax.sharding import Mesh, PartitionSpec as P

D = 8192
QH = 32
KVH = 4
HD = 128
PROMPT = 1024
NPROMPT = 4
RESP = 128
ROWS = 64
EPS = 1e-06
F32 = jnp.float32
BF16 = jnp.bfloat16
VMEM = 12 * 1024 * 1024
BRIEF = pl.CostEstimate(flops=1, bytes_accessed=1, transcendentals=0)

PLACES = ((0, 0), (1, 0), (0, 3), (0, 1), (0, 2), (1, 2), (1, 3), (1, 1))


def shift(value, axis, by):
    size = lax.axis_size(axis)
    return lax.ppermute(value, axis, [(i, (i + by) % size) for i in range(size)])


def params(**kw):
    return pltpu.CompilerParams(vmem_limit_bytes=VMEM, **kw)


def norm_kernel(x_ref, gain_ref, out_ref):
    wide = x_ref[...].astype(F32)
    mean = jnp.mean(wide * wide, axis=-1, keepdims=True)
    out_ref[...] = (wide * lax.rsqrt(mean + EPS) * gain_ref[...]).astype(BF16)


def norm(hidden, gain):
    return pl.pallas_call(
        norm_kernel,
        out_shape=jax.ShapeDtypeStruct((ROWS, D), BF16),
        grid=(2,),
        in_specs=[
            pl.BlockSpec((ROWS // 2, D), lambda i: (i, 0)),
            pl.BlockSpec((1, D), lambda i: (0, 0)),
        ],
        out_specs=pl.BlockSpec((ROWS // 2, D), lambda i: (i, 0)),
        compiler_params=params(),
        cost_estimate=BRIEF,
        name="norm",
    )(hidden, gain)


def turned(value, cosines, sines):
    return value * cosines + pltpu.roll(value, HD // 2, 1) * sines


def merge_kernel(places, *refs):
    out_ref, sems = refs[-2:]
    copies = [
        pltpu.make_async_copy(refs[source].at[there], out_ref.at[here], sems.at[i])
        for i, (source, there, here) in enumerate(places)
    ]
    for copy in copies:
        copy.start()
    for copy in copies:
        copy.wait()


def merge(own, other, shape, places):
    hbm = pl.BlockSpec(memory_space=pl.ANY)
    return pl.pallas_call(
        functools.partial(merge_kernel, places),
        out_shape=jax.ShapeDtypeStruct(shape, BF16),
        in_specs=[hbm, hbm],
        out_specs=pl.BlockSpec(memory_space=pltpu.VMEM),
        scratch_shapes=[pltpu.SemaphoreType.DMA((len(places),))],
        compiler_params=params(),
        cost_estimate=BRIEF,
        name="merge",
    )(own, other)


def merge_columns(own, other):
    rows, cols = own.shape
    every = slice(None)
    places = [
        (i, (every, every), (every, slice(i * cols, (i + 1) * cols))) for i in range(2)
    ]
    return merge(own, other, (rows, 2 * cols), places)


def merge_rows(own, other):
    rows, cols = own.shape
    every = slice(None)
    places = [
        (i, (every, every), (slice(i * rows, (i + 1) * rows), every)) for i in range(2)
    ]
    return merge(own, other, (2 * rows, cols), places)


def merge_cache(own, other):
    every = slice(None)
    places = [
        (i, (every, p), (p, slice(8 * i, 8 * (i + 1)))) for i in range(2) for p in range(NPROMPT)
    ]
    return merge(own, other, (NPROMPT, 16, ROWS, 2 * HD), places)


def query_kernel(count, *refs):
    pieces = refs[:count]
    w_ref, cos_ref, sin_ref, out_ref = refs[count:]
    depth = D // 2
    total = None
    for step in range(2):
        part = slice(step * depth, (step + 1) * depth)
        rows = jnp.concatenate([piece[:, part] for piece in pieces], axis=0)
        term = jnp.dot(rows, w_ref[part, :], preferred_element_type=F32)
        total = term if total is None else total + term
    for block in range(out_ref.shape[0]):
        for head in range(4):
            part = total[block * ROWS : (block + 1) * ROWS, head * HD : (head + 1) * HD]
            out_ref[block, head * ROWS : (head + 1) * ROWS, :] = turned(
                part, cos_ref[...], sin_ref[...]
            ).astype(BF16)


def project_queries(pieces, weight, cosines, sines):
    rows = sum(piece.shape[0] for piece in pieces)
    return pl.pallas_call(
        functools.partial(query_kernel, len(pieces)),
        out_shape=jax.ShapeDtypeStruct((rows // ROWS, 4 * ROWS, HD), BF16),
        compiler_params=params(),
        cost_estimate=BRIEF,
        name="queries",
    )(*pieces, weight, cosines, sines)


def dot_t(a, b):
    return lax.dot_general(a, b, (((1,), (1,)), ((), ())), preferred_element_type=F32)


def pair_kernel(count, *refs):
    pieces = refs[:count]
    core_ref, w_ref, cos_ref, sin_ref, out_ref = refs[count:]
    depth = D // 2
    total = None
    for step in range(2):
        part = slice(step * depth, (step + 1) * depth)
        rows = jnp.concatenate([piece[:, part] for piece in pieces], axis=0)
        term = dot_t(rows, w_ref[:, part])
        total = term if total is None else total + term
    pairs = total.astype(BF16).astype(F32)
    pairs = jnp.where(core_ref[0] == 0, pairs, pltpu.roll(pairs, HD // 2, 1))
    for block in range(out_ref.shape[0]):
        part = pairs[block * ROWS : (block + 1) * ROWS, :]
        out_ref[block] = turned(part, cos_ref[...], sin_ref[...]).astype(BF16)


def project_pairs(pieces, core, weight, cosines, sines):
    rows = sum(piece.shape[0] for piece in pieces)
    vmem = pl.BlockSpec(memory_space=pltpu.VMEM)
    return pl.pallas_call(
        functools.partial(pair_kernel, len(pieces)),
        out_shape=jax.ShapeDtypeStruct((rows // ROWS, ROWS, HD), BF16),
        in_specs=[vmem] * len(pieces) + [pl.BlockSpec(memory_space=pltpu.SMEM)] + [vmem] * 3,
        compiler_params=params(),
        cost_estimate=BRIEF,
        name="pairs",
    )(*pieces, core, weight, cosines, sines)


def sort_kernel(key_ref, value_ref, out_ref):
    out_ref[0, :, :, :HD] = key_ref[...]
    out_ref[0, :, :, HD:] = value_ref[...]


def sort_cache(cache):
    return pl.pallas_call(
        sort_kernel,
        out_shape=jax.ShapeDtypeStruct((2 * KVH, NPROMPT, ROWS, 2 * HD), BF16),
        grid=(2 * KVH,),
        in_specs=[
            pl.BlockSpec((NPROMPT, ROWS, HD), lambda i: (0, 0, i // 2)),
            pl.BlockSpec((NPROMPT, ROWS, HD), lambda i: (0, 0, KVH + i // 2)),
        ],
        out_specs=pl.BlockSpec((1, NPROMPT, ROWS, 2 * HD), lambda i: (i, 0, 0, 0)),
        compiler_params=params(),
        cost_estimate=BRIEF,
        name="sort_cache",
    )(cache, cache)


def prompt_kernel(prompt_ref, q_ref, cache_ref, acc_ref, state_ref):
    lane = lax.broadcasted_iota(jnp.int32, (4 * ROWS, HD), 1)

    @pl.loop(0, q_ref.shape[0])
    def _(i):
        cache = cache_ref[prompt_ref[i]].reshape(PROMPT, 2 * HD)
        scores = dot_t(q_ref[i], cache[:, :HD]) * HD ** (-0.5)
        top = jnp.max(scores, axis=-1, keepdims=True)
        probs = jnp.exp(scores - top)
        total = jnp.sum(probs, axis=-1, keepdims=True)
        acc_ref[i] = jnp.dot(probs.astype(BF16), cache[:, HD:], preferred_element_type=F32)
        state_ref[i] = jnp.where(lane < HD // 2, top, total)


def attend_prompt(queries, cache, prompts):
    shape = jax.ShapeDtypeStruct(queries.shape, F32)
    vmem = pl.BlockSpec(memory_space=pltpu.VMEM)
    return pl.pallas_call(
        prompt_kernel,
        out_shape=(shape, shape),
        in_specs=[pl.BlockSpec(memory_space=pltpu.SMEM), vmem, vmem],
        compiler_params=params(),
        cost_estimate=BRIEF,
        name="attend_prompt",
    )(prompts, queries, cache)


def own_kernel(info_ref, q_ref, acc_ref, state_ref, own_ref, other_ref, out_ref):
    lane = lax.broadcasted_iota(jnp.int32, (4 * ROWS, HD), 1)
    line = lax.broadcasted_iota(jnp.int32, (4 * ROWS, HD), 0) % ROWS

    @pl.loop(0, q_ref.shape[0])
    def _(i):
        length, core, kind = info_ref[0, i], info_ref[1, i], info_ref[2, i]
        key_at, value_at = info_ref[3, i], info_ref[4, i]
        keys = jnp.concatenate([own_ref[kind, key_at], other_ref[kind, key_at]], axis=0)
        values = jnp.concatenate(
            [own_ref[1 - kind, value_at], other_ref[1 - kind, value_at]], axis=0
        )
        scores = dot_t(q_ref[i], keys) * HD ** (-0.5)
        row = line + core * ROWS
        place = jnp.where(lane < ROWS, lane + core * ROWS, lane - core * ROWS)
        visible = (place <= row) & (place < length)
        scores = jnp.where(visible, scores, -jnp.inf)
        state = state_ref[i]
        top_a = state[:, :1]
        total_a = state[:, HD // 2 : HD // 2 + 1]
        top = jnp.maximum(top_a, jnp.max(scores, axis=-1, keepdims=True))
        scale = jnp.exp(top_a - top)
        probs = jnp.exp(scores - top)
        total = total_a * scale + jnp.sum(probs, axis=-1, keepdims=True)
        blended = acc_ref[i] * scale + jnp.dot(
            probs.astype(BF16), values, preferred_element_type=F32
        )
        blended = jnp.where(row < length, blended / total, 0.0).astype(BF16)
        for head in range(4):
            out_ref[i, :, head * HD : (head + 1) * HD] = blended[
                head * ROWS : (head + 1) * ROWS, :
            ]


def attend_own(queries, acc, state, pairs_own, pairs_other, info):
    count = queries.shape[0]
    vmem = pl.BlockSpec(memory_space=pltpu.VMEM)
    out = pl.pallas_call(
        own_kernel,
        out_shape=jax.ShapeDtypeStruct((count, ROWS, 4 * HD), BF16),
        in_specs=[pl.BlockSpec(memory_space=pltpu.SMEM)] + [vmem] * 5,
        compiler_params=params(),
        cost_estimate=BRIEF,
        name="attend_own",
    )(info, queries, acc, state, pairs_own, pairs_other)
    return out.reshape(count * ROWS, 4 * HD)


def output_kernel(counts, x_ref, w_ref, *out_refs):
    tile = 1024

    @pl.loop(0, D // 2 // tile)
    def _(step):
        inner = pl.ds(pl.multiple_of(step * tile, tile), tile)
        for side in range(2):
            part = pl.ds(pl.multiple_of(side * (D // 2) + step * tile, tile), tile)
            total = jnp.dot(x_ref[...], w_ref[:, part], preferred_element_type=F32)
            total = total.astype(BF16)
            at = 0
            for block, count in enumerate(counts):
                rows = total[block * ROWS : (block + 1) * ROWS, :]
                if count == 1:
                    out_refs[at][:, part] = rows
                else:
                    out_refs[at + side][:, inner] = rows
                at += count


def project_out(attended, weight, counts):
    return pl.pallas_call(
        functools.partial(output_kernel, counts),
        out_shape=[
            jax.ShapeDtypeStruct((ROWS, D // count), BF16) for count in counts for _ in range(count)
        ],
        compiler_params=params(),
        cost_estimate=BRIEF,
        name="project_out",
    )(attended, weight)


def sum_kernel(start, *refs):
    width = refs[-1].shape[1]
    total = 0.0
    for ref in refs[:-1]:
        low = start if ref.shape[1] > width else 0
        total += ref[:, low : low + width].astype(F32)
    refs[-1][...] = total.astype(BF16)


def split_kernel(a_ref, b_ref, low_ref, high_ref):
    total = (a_ref[...].astype(F32) + b_ref[...].astype(F32)).astype(BF16)
    half = low_ref.shape[1]
    low_ref[...] = total[:, :half]
    high_ref[...] = total[:, half:]


def split_sum(a, b):
    half = jax.ShapeDtypeStruct((a.shape[0], a.shape[1] // 2), BF16)
    return pl.pallas_call(
        split_kernel,
        out_shape=(half, half),
        compiler_params=params(),
        cost_estimate=BRIEF,
        name="split_sum",
    )(a, b)


def relay_kernel(a_ref, up_ref, b_ref, down_ref, a_out, b_out):
    half = up_ref.shape[1]
    a_out[:, :half] = (a_ref[:, :half].astype(F32) + up_ref[...].astype(F32)).astype(BF16)
    a_out[:, half:] = a_ref[:, half:]
    b_out[:, :half] = b_ref[:, :half]
    b_out[:, half:] = (b_ref[:, half:].astype(F32) + down_ref[...].astype(F32)).astype(BF16)


def relay_sum(a, up, b, down):
    whole = jax.ShapeDtypeStruct(a.shape, BF16)
    return pl.pallas_call(
        relay_kernel,
        out_shape=(whole, whole),
        compiler_params=params(),
        cost_estimate=BRIEF,
        name="relay_sum",
    )(a, up, b, down)


def add(*terms, start=0):
    width = min(term.shape[1] for term in terms)
    return pl.pallas_call(
        functools.partial(sum_kernel, start),
        out_shape=jax.ShapeDtypeStruct((terms[0].shape[0], width), BF16),
        compiler_params=params(),
        cost_estimate=BRIEF,
        name="add",
    )(*terms)


def after(value, *others):
    return lax.optimization_barrier((value, *others))[0]


def rope_tables():
    half = HD // 2
    position = (PROMPT + jnp.arange(RESP)).astype(F32)
    inverse = jnp.exp(-(2.0 * jnp.arange(half).astype(F32) / HD) * jnp.log(10000.0))
    angles = position[:, None] * inverse[None, :]
    cosines, sines = jnp.cos(angles), jnp.sin(angles)
    return (
        jnp.concatenate([cosines, cosines], axis=1),
        jnp.concatenate([-sines, sines], axis=1),
    )


def body(hidden, norm_gain, query_weight, kv_weight, out_weight, prompt_cache, resp_len, prompt_id):
    xh, y, core = lax.axis_index("xh"), lax.axis_index("y"), lax.axis_index("c")
    wq, wkv, wo = query_weight[0], kv_weight[0].T, out_weight[0]
    chips = ("xh", "y")

    normed = norm(hidden, norm_gain)
    b10 = shift(normed, "xh", 1)
    b03 = shift(normed, "y", 1)
    b01 = shift(normed, "y", -1)
    wq_other = shift(wq, "c", 1)
    wo_other = shift(wo, "c", 1)
    wkv_other = shift(after(wkv, wq_other), "c", 1)
    cache = sort_cache(after(prompt_cache[0], normed))
    cache = lax.all_to_all(cache, chips, 0, 0, tiled=True)

    cosines, sines = rope_tables()
    cosines = lax.dynamic_slice_in_dim(cosines, core * ROWS, ROWS, 0)
    sines = lax.dynamic_slice_in_dim(sines, core * ROWS, ROWS, 0)
    key_cosines = jnp.where(xh == 0, cosines, 1.0)
    key_sines = jnp.where(xh == 0, sines, 0.0)

    def pick(values, index):
        lanes = jnp.arange(8)
        return jnp.sum(jnp.where(index[:, None] == lanes[None, :], values[None, :], 0), axis=1)

    responses = jnp.stack([(xh ^ dx) * 4 + (y + dy) % 4 for dx, dy in PLACES])
    prompts = pick(prompt_id, responses).astype(jnp.int32)
    lengths = pick(resp_len, responses)
    maker_y = xh * 2 + y // 2
    table = [0] * 8
    for at, (dx, dy) in enumerate(PLACES):
        table[dx * 4 + dy] = at
    table = jnp.array(table, jnp.int32)
    away = (responses % 4 - maker_y) % 4
    key_at = pick(table, (responses // 4) * 4 + away)
    value_at = pick(table, (1 - responses // 4) * 4 + away)
    info = jnp.stack(
        [
            lengths,
            jnp.full((8,), core, jnp.int32),
            jnp.full((8,), y % 2, jnp.int32),
            key_at,
            value_at,
        ]
    ).astype(jnp.int32)
    core_word = jnp.full((1,), core, jnp.int32)

    b03 = after(b03, b10, wq_other, wo_other, info, prompts, key_cosines, key_sines, core_word)
    b01 = after(b01, b03, cache)
    upper, lower = b03[: ROWS // 2], b01[ROWS // 2 :]
    top02 = shift(upper, "y", 1)
    low02 = shift(lower, "y", -1)
    b02 = jnp.concatenate([top02, low02], axis=0)
    b12 = shift(b02, "xh", 1)
    b10 = after(b10, b02)
    b13 = shift(b10, "y", 1)
    b11 = shift(b10, "y", -1)
    cache = after(cache, b02)
    cache = merge_cache(cache, shift(cache, "c", 1))
    wkv = merge_rows(after(wkv, b02), wkv_other)
    wq = merge_columns(after(wq, b02), wq_other)

    near = [normed, b10, b03, b01, b02]
    far = [b12, b13, b11]
    pairs_near = project_pairs(near, core_word, wkv, key_cosines, key_sines)
    q_near = project_queries(near, wq, cosines, sines)
    acc_near, state_near = attend_prompt(q_near, cache, prompts[:5])
    wo = merge_rows(after(wo, acc_near), wo_other)
    far[0] = after(far[0], pairs_near, wo)
    pairs_far = project_pairs(far, core_word, wkv, key_cosines, key_sines)
    pairs = jnp.concatenate([pairs_near, pairs_far], axis=0)
    straight = [(g, 2 * g) for g in range(4)] + [(4 + g, 2 * g + 1) for g in range(4)]
    crossed = [(g, 2 * g + 1) for g in range(4)] + [(4 + g, 2 * g) for g in range(4)]
    first, second = lax.ppermute(pairs, chips, straight), lax.ppermute(pairs, chips, crossed)
    far[0] = after(far[0], pairs_far)
    q_far = project_queries(far, wq, cosines, sines)
    pairs = jnp.stack([after(first, q_far), second])
    pairs_other = shift(pairs, "c", 1)
    acc, state = attend_prompt(q_far, cache, prompts[5:])
    pairs_other = after(pairs_other, acc)
    att_far = attend_own(q_far, acc, state, pairs, pairs_other, info[:, 5:])

    p12b, p12a, p13, p11 = project_out(att_far, wo, (2, 1, 1))
    across_a = shift(p12a, "xh", 1)
    up = shift(p11, "y", 1)
    down = shift(p13, "y", -1)
    across_b = shift(p12b, "xh", 1)
    att_near = attend_own(
        q_near, acc_near, state_near, after(pairs, p11), pairs_other, info[:, :5]
    )
    p00, p10, p03b, p03a, p01b, p01a, p02b, p02a = project_out(att_near, wo, (1, 1, 2, 2, 2))
    up_a, down_a = split_sum(p02a, across_a)
    across = add(after(p10, up_a), up, down)
    up_b, down_b = split_sum(after(p02b, across), across_b)
    p01a = after(p01a, up_b)
    up_a, down_a = shift(up_a, "y", 1), shift(down_a, "y", -1)
    across = shift(across, "xh", 1)
    up_b, down_b = shift(up_b, "y", 1), shift(down_b, "y", -1)
    p01a, p03a = relay_sum(p01a, up_a, p03a, down_a)
    up_a, down_a = shift(p01a, "y", 1), shift(p03a, "y", -1)
    p01b, p03b = relay_sum(after(p01b, p01a), up_b, p03b, down_b)
    up_b, down_b = shift(p01b, "y", 1), shift(p03b, "y", -1)
    onward = [(i, (i + 1) % 16) for i in range(16)]
    total_a = add(hidden, p00, across, up_a, down_a, start=D // 2)
    total_b = add(after(hidden, total_a), p00, across, up_b, down_b)
    out_a = lax.ppermute(total_a, ("xl", "z"), onward)
    out_b = lax.ppermute(total_b, ("xl", "z"), onward)
    return jnp.concatenate([out_b, out_a], axis=1)


def solution(mesh):
    whole = Mesh(mesh.devices.reshape(2, 8, 2, 4, 2), ("xl", "z", "xh", "y", "c"))
    section, tp = ("xl", "z"), ("xh", "y", "c")
    in_specs = (
        P(section + tp, None),
        P(section, None),
        P(section, None, tp),
        P(section, None, tp),
        P(section, tp, None),
        P(section, None, tp, None),
        P(section),
        P(section),
    )
    out_specs = P(section + tp, None)
    return jax.shard_map(body, mesh=whole, in_specs=in_specs, out_specs=out_specs, check_vma=False)
```

```python
import functools

import jax
import jax.numpy as jnp
from jax import lax
from jax.experimental import pallas as pl
from jax.experimental.pallas import tpu as pltpu
from jax.sharding import Mesh, PartitionSpec as P

D = 8192
QH = 32
KVH = 4
HD = 128
PROMPT = 1024
NPROMPT = 4
RESP = 128
ROWS = 64
EPS = 1e-06
F32 = jnp.float32
BF16 = jnp.bfloat16
VMEM = 12 * 1024 * 1024
BRIEF = pl.CostEstimate(flops=1, bytes_accessed=1, transcendentals=0)

PLACES = ((0, 0), (1, 0), (0, 3), (0, 1), (0, 2), (1, 3), (1, 1), (1, 2))


def shift(value, axis, by):
    size = lax.axis_size(axis)
    return lax.ppermute(value, axis, [(i, (i + by) % size) for i in range(size)])


def params(**kw):
    return pltpu.CompilerParams(vmem_limit_bytes=VMEM, **kw)


def norm_kernel(x_ref, gain_ref, out_ref):
    wide = x_ref[...].astype(F32)
    mean = jnp.mean(wide * wide, axis=-1, keepdims=True)
    out_ref[...] = (wide * lax.rsqrt(mean + EPS) * gain_ref[...]).astype(BF16)


def norm(hidden, gain):
    return pl.pallas_call(
        norm_kernel,
        out_shape=jax.ShapeDtypeStruct((ROWS, D), BF16),
        grid=(2,),
        in_specs=[
            pl.BlockSpec((ROWS // 2, D), lambda i: (i, 0)),
            pl.BlockSpec((1, D), lambda i: (0, 0)),
        ],
        out_specs=pl.BlockSpec((ROWS // 2, D), lambda i: (i, 0)),
        compiler_params=params(),
        cost_estimate=BRIEF,
        name="norm",
    )(hidden, gain)


def turned(value, cosines, sines):
    return value * cosines + pltpu.roll(value, HD // 2, 1) * sines


def merge_kernel(places, *refs):
    out_ref, sems = refs[-2:]
    copies = [
        pltpu.make_async_copy(refs[source].at[there], out_ref.at[here], sems.at[i])
        for i, (source, there, here) in enumerate(places)
    ]
    for copy in copies:
        copy.start()
    for copy in copies:
        copy.wait()


def merge(own, other, shape, places):
    hbm = pl.BlockSpec(memory_space=pl.ANY)
    return pl.pallas_call(
        functools.partial(merge_kernel, places),
        out_shape=jax.ShapeDtypeStruct(shape, BF16),
        in_specs=[hbm, hbm],
        out_specs=pl.BlockSpec(memory_space=pltpu.VMEM),
        scratch_shapes=[pltpu.SemaphoreType.DMA((len(places),))],
        compiler_params=params(),
        cost_estimate=BRIEF,
        name="merge",
    )(own, other)


def merge_columns(own, other):
    rows, cols = own.shape
    every = slice(None)
    places = [
        (i, (every, every), (every, slice(i * cols, (i + 1) * cols))) for i in range(2)
    ]
    return merge(own, other, (rows, 2 * cols), places)


def merge_rows(own, other):
    rows, cols = own.shape
    every = slice(None)
    places = [
        (i, (every, every), (slice(i * rows, (i + 1) * rows), every)) for i in range(2)
    ]
    return merge(own, other, (2 * rows, cols), places)


def merge_cache(own, other):
    every = slice(None)
    places = [
        (i, (every, p), (p, slice(8 * i, 8 * (i + 1)))) for i in range(2) for p in range(NPROMPT)
    ]
    return merge(own, other, (NPROMPT, 16, ROWS, 2 * HD), places)


def query_kernel(count, *refs):
    pieces = refs[:count]
    w_ref, cos_ref, sin_ref, out_ref = refs[count:]
    depth = D // 2
    total = None
    for step in range(2):
        part = slice(step * depth, (step + 1) * depth)
        rows = jnp.concatenate([piece[:, part] for piece in pieces], axis=0)
        term = jnp.dot(rows, w_ref[part, :], preferred_element_type=F32)
        total = term if total is None else total + term
    for block in range(out_ref.shape[0]):
        for head in range(4):
            part = total[block * ROWS : (block + 1) * ROWS, head * HD : (head + 1) * HD]
            out_ref[block, head * ROWS : (head + 1) * ROWS, :] = turned(
                part, cos_ref[...], sin_ref[...]
            ).astype(BF16)


def project_queries(pieces, weight, cosines, sines):
    rows = sum(piece.shape[0] for piece in pieces)
    return pl.pallas_call(
        functools.partial(query_kernel, len(pieces)),
        out_shape=jax.ShapeDtypeStruct((rows // ROWS, 4 * ROWS, HD), BF16),
        compiler_params=params(),
        cost_estimate=BRIEF,
        name="queries",
    )(*pieces, weight, cosines, sines)


def dot_t(a, b):
    return lax.dot_general(a, b, (((1,), (1,)), ((), ())), preferred_element_type=F32)


def pair_kernel(count, *refs):
    pieces = refs[:count]
    core_ref, w_ref, cos_ref, sin_ref, out_ref = refs[count:]
    depth = D // 2
    total = None
    for step in range(2):
        part = slice(step * depth, (step + 1) * depth)
        rows = jnp.concatenate([piece[:, part] for piece in pieces], axis=0)
        term = dot_t(rows, w_ref[:, part])
        total = term if total is None else total + term
    pairs = total.astype(BF16).astype(F32)
    pairs = jnp.where(core_ref[0] == 0, pairs, pltpu.roll(pairs, HD // 2, 1))
    for block in range(out_ref.shape[0]):
        part = pairs[block * ROWS : (block + 1) * ROWS, :]
        out_ref[block] = turned(part, cos_ref[...], sin_ref[...]).astype(BF16)


def project_pairs(pieces, core, weight, cosines, sines):
    rows = sum(piece.shape[0] for piece in pieces)
    vmem = pl.BlockSpec(memory_space=pltpu.VMEM)
    return pl.pallas_call(
        functools.partial(pair_kernel, len(pieces)),
        out_shape=jax.ShapeDtypeStruct((rows // ROWS, ROWS, HD), BF16),
        in_specs=[vmem] * len(pieces) + [pl.BlockSpec(memory_space=pltpu.SMEM)] + [vmem] * 3,
        compiler_params=params(),
        cost_estimate=BRIEF,
        name="pairs",
    )(*pieces, core, weight, cosines, sines)


def sort_kernel(key_ref, value_ref, out_ref):
    out_ref[0, :, :, :HD] = key_ref[...]
    out_ref[0, :, :, HD:] = value_ref[...]


def sort_cache(cache):
    return pl.pallas_call(
        sort_kernel,
        out_shape=jax.ShapeDtypeStruct((2 * KVH, NPROMPT, ROWS, 2 * HD), BF16),
        grid=(2 * KVH,),
        in_specs=[
            pl.BlockSpec((NPROMPT, ROWS, HD), lambda i: (0, 0, i // 2)),
            pl.BlockSpec((NPROMPT, ROWS, HD), lambda i: (0, 0, KVH + i // 2)),
        ],
        out_specs=pl.BlockSpec((1, NPROMPT, ROWS, 2 * HD), lambda i: (i, 0, 0, 0)),
        compiler_params=params(),
        cost_estimate=BRIEF,
        name="sort_cache",
    )(cache, cache)


def prompt_kernel(prompt_ref, q_ref, cache_ref, acc_ref, state_ref):
    lane = lax.broadcasted_iota(jnp.int32, (4 * ROWS, HD), 1)

    @pl.loop(0, q_ref.shape[0])
    def _(i):
        cache = cache_ref[prompt_ref[i]].reshape(PROMPT, 2 * HD)
        scores = dot_t(q_ref[i], cache[:, :HD]) * HD ** (-0.5)
        top = jnp.max(scores, axis=-1, keepdims=True)
        probs = jnp.exp(scores - top)
        total = jnp.sum(probs, axis=-1, keepdims=True)
        acc_ref[i] = jnp.dot(probs.astype(BF16), cache[:, HD:], preferred_element_type=F32)
        state_ref[i] = jnp.where(lane < HD // 2, top, total)


def attend_prompt(queries, cache, prompts):
    shape = jax.ShapeDtypeStruct(queries.shape, F32)
    vmem = pl.BlockSpec(memory_space=pltpu.VMEM)
    return pl.pallas_call(
        prompt_kernel,
        out_shape=(shape, shape),
        in_specs=[pl.BlockSpec(memory_space=pltpu.SMEM), vmem, vmem],
        compiler_params=params(),
        cost_estimate=BRIEF,
        name="attend_prompt",
    )(prompts, queries, cache)


def own_kernel(info_ref, q_ref, acc_ref, state_ref, own_ref, other_ref, out_ref):
    lane = lax.broadcasted_iota(jnp.int32, (4 * ROWS, HD), 1)
    line = lax.broadcasted_iota(jnp.int32, (4 * ROWS, HD), 0) % ROWS

    @pl.loop(0, q_ref.shape[0])
    def _(i):
        length, core, kind = info_ref[0, i], info_ref[1, i], info_ref[2, i]
        key_at, value_at = info_ref[3, i], info_ref[4, i]
        keys = jnp.concatenate([own_ref[kind, key_at], other_ref[kind, key_at]], axis=0)
        values = jnp.concatenate(
            [own_ref[1 - kind, value_at], other_ref[1 - kind, value_at]], axis=0
        )
        scores = dot_t(q_ref[i], keys) * HD ** (-0.5)
        row = line + core * ROWS
        place = jnp.where(lane < ROWS, lane + core * ROWS, lane - core * ROWS)
        visible = (place <= row) & (place < length)
        scores = jnp.where(visible, scores, -jnp.inf)
        state = state_ref[i]
        top_a = state[:, :1]
        total_a = state[:, HD // 2 : HD // 2 + 1]
        top = jnp.maximum(top_a, jnp.max(scores, axis=-1, keepdims=True))
        scale = jnp.exp(top_a - top)
        probs = jnp.exp(scores - top)
        total = total_a * scale + jnp.sum(probs, axis=-1, keepdims=True)
        blended = acc_ref[i] * scale + jnp.dot(
            probs.astype(BF16), values, preferred_element_type=F32
        )
        blended = jnp.where(row < length, blended / total, 0.0).astype(BF16)
        for head in range(4):
            out_ref[i, :, head * HD : (head + 1) * HD] = blended[
                head * ROWS : (head + 1) * ROWS, :
            ]


def attend_own(queries, acc, state, pairs_own, pairs_other, info):
    count = queries.shape[0]
    vmem = pl.BlockSpec(memory_space=pltpu.VMEM)
    out = pl.pallas_call(
        own_kernel,
        out_shape=jax.ShapeDtypeStruct((count, ROWS, 4 * HD), BF16),
        in_specs=[pl.BlockSpec(memory_space=pltpu.SMEM)] + [vmem] * 5,
        compiler_params=params(),
        cost_estimate=BRIEF,
        name="attend_own",
    )(info, queries, acc, state, pairs_own, pairs_other)
    return out.reshape(count * ROWS, 4 * HD)


def output_kernel(counts, x_ref, w_ref, *out_refs):
    tile = 1024

    @pl.loop(0, D // 2 // tile)
    def _(step):
        inner = pl.ds(pl.multiple_of(step * tile, tile), tile)
        for side in range(2):
            part = pl.ds(pl.multiple_of(side * (D // 2) + step * tile, tile), tile)
            total = jnp.dot(x_ref[...], w_ref[:, part], preferred_element_type=F32)
            total = total.astype(BF16)
            at = 0
            for block, count in enumerate(counts):
                rows = total[block * ROWS : (block + 1) * ROWS, :]
                if count == 1:
                    out_refs[at][:, part] = rows
                else:
                    out_refs[at + side][:, inner] = rows
                at += count


def project_out(attended, weight, counts):
    return pl.pallas_call(
        functools.partial(output_kernel, counts),
        out_shape=[
            jax.ShapeDtypeStruct((ROWS, D // count), BF16) for count in counts for _ in range(count)
        ],
        compiler_params=params(),
        cost_estimate=BRIEF,
        name="project_out",
    )(attended, weight)


def sum_kernel(start, *refs):
    width = refs[-1].shape[1]
    total = 0.0
    for ref in refs[:-1]:
        low = start if ref.shape[1] > width else 0
        total += ref[:, low : low + width].astype(F32)
    refs[-1][...] = total.astype(BF16)


def split_kernel(a_ref, b_ref, low_ref, high_ref):
    total = (a_ref[...].astype(F32) + b_ref[...].astype(F32)).astype(BF16)
    half = low_ref.shape[1]
    low_ref[...] = total[:, :half]
    high_ref[...] = total[:, half:]


def split_sum(a, b):
    half = jax.ShapeDtypeStruct((a.shape[0], a.shape[1] // 2), BF16)
    return pl.pallas_call(
        split_kernel,
        out_shape=(half, half),
        compiler_params=params(),
        cost_estimate=BRIEF,
        name="split_sum",
    )(a, b)


def place_kernel(start, *refs):
    value_ref, out_ref, sem = refs[-3:]
    width = value_ref.shape[1]
    copy = pltpu.make_async_copy(value_ref, out_ref.at[:, pl.ds(start, width)], sem)
    copy.start()
    copy.wait()


def place(value, start, whole=None):
    hbm = pl.BlockSpec(memory_space=pl.ANY)
    given = () if whole is None else (whole,)
    return pl.pallas_call(
        functools.partial(place_kernel, start),
        out_shape=jax.ShapeDtypeStruct((ROWS, D), BF16),
        in_specs=[hbm] * (len(given) + 1),
        out_specs=hbm,
        scratch_shapes=[pltpu.SemaphoreType.DMA],
        input_output_aliases={0: 0} if given else {},
        compiler_params=params(),
        cost_estimate=BRIEF,
        name="place",
    )(*given, value)


def relay_kernel(a_ref, up_ref, b_ref, down_ref, a_out, b_out):
    half = up_ref.shape[1]
    a_out[:, :half] = (a_ref[:, :half].astype(F32) + up_ref[...].astype(F32)).astype(BF16)
    a_out[:, half:] = a_ref[:, half:]
    b_out[:, :half] = b_ref[:, :half]
    b_out[:, half:] = (b_ref[:, half:].astype(F32) + down_ref[...].astype(F32)).astype(BF16)


def relay_sum(a, up, b, down):
    whole = jax.ShapeDtypeStruct(a.shape, BF16)
    return pl.pallas_call(
        relay_kernel,
        out_shape=(whole, whole),
        compiler_params=params(),
        cost_estimate=BRIEF,
        name="relay_sum",
    )(a, up, b, down)


def add(*terms, start=0):
    width = min(term.shape[1] for term in terms)
    return pl.pallas_call(
        functools.partial(sum_kernel, start),
        out_shape=jax.ShapeDtypeStruct((terms[0].shape[0], width), BF16),
        compiler_params=params(),
        cost_estimate=BRIEF,
        name="add",
    )(*terms)


def after(value, *others):
    return lax.optimization_barrier((value, *others))[0]


def rope_tables():
    half = HD // 2
    position = (PROMPT + jnp.arange(RESP)).astype(F32)
    inverse = jnp.exp(-(2.0 * jnp.arange(half).astype(F32) / HD) * jnp.log(10000.0))
    angles = position[:, None] * inverse[None, :]
    cosines, sines = jnp.cos(angles), jnp.sin(angles)
    return (
        jnp.concatenate([cosines, cosines], axis=1),
        jnp.concatenate([-sines, sines], axis=1),
    )


def body(hidden, norm_gain, query_weight, kv_weight, out_weight, prompt_cache, resp_len, prompt_id):
    xh, y, core = lax.axis_index("xh"), lax.axis_index("y"), lax.axis_index("c")
    wq, wkv, wo = query_weight[0], kv_weight[0].T, out_weight[0]
    chips = ("xh", "y")

    normed = norm(hidden, norm_gain)
    b10 = shift(normed, "xh", 1)
    b03 = shift(normed, "y", 1)
    b01 = shift(normed, "y", -1)
    wkv_other = shift(wkv, "c", 1)
    wq_other = shift(wq, "c", 1)
    cache = sort_cache(after(prompt_cache[0], normed))
    cache = lax.all_to_all(cache, chips, 0, 0, tiled=True)

    cosines, sines = rope_tables()
    cosines = lax.dynamic_slice_in_dim(cosines, core * ROWS, ROWS, 0)
    sines = lax.dynamic_slice_in_dim(sines, core * ROWS, ROWS, 0)
    key_cosines = jnp.where(xh == 0, cosines, 1.0)
    key_sines = jnp.where(xh == 0, sines, 0.0)

    def pick(values, index):
        lanes = jnp.arange(8)
        return jnp.sum(jnp.where(index[:, None] == lanes[None, :], values[None, :], 0), axis=1)

    responses = jnp.stack([(xh ^ dx) * 4 + (y + dy) % 4 for dx, dy in PLACES])
    prompts = pick(prompt_id, responses).astype(jnp.int32)
    lengths = pick(resp_len, responses)
    maker_y = xh * 2 + y // 2
    table = [0] * 8
    for at, (dx, dy) in enumerate(PLACES):
        table[dx * 4 + dy] = at
    table = jnp.array(table, jnp.int32)
    away = (responses % 4 - maker_y) % 4
    key_at = pick(table, (responses // 4) * 4 + away)
    value_at = pick(table, (1 - responses // 4) * 4 + away)
    info = jnp.stack(
        [
            lengths,
            jnp.full((8,), core, jnp.int32),
            jnp.full((8,), y % 2, jnp.int32),
            key_at,
            value_at,
        ]
    ).astype(jnp.int32)
    core_word = jnp.full((1,), core, jnp.int32)

    b03 = after(b03, b10, wq_other, wkv_other, info, prompts, key_cosines, key_sines, core_word)
    b01 = after(b01, b03, cache)
    upper, lower = b03[: ROWS // 2], b01[ROWS // 2 :]
    top02 = shift(upper, "y", 1)
    low02 = shift(lower, "y", -1)
    wkv = merge_rows(after(wkv, lower), wkv_other)
    wq = merge_columns(after(wq, lower), wq_other)
    b02 = jnp.concatenate([after(top02, wkv, wq), low02], axis=0)
    b12 = shift(b02, "xh", 1)
    b10 = after(b10, lower)
    b13 = shift(b10, "y", 1)
    b11 = shift(b10, "y", -1)
    cache = after(cache, lower)
    cache = merge_cache(cache, shift(cache, "c", 1))

    near = [normed, b10, b03, b01, b02]
    far = [b13, b11, b12]
    pairs_near = project_pairs(near, core_word, wkv, key_cosines, key_sines)
    q_near = project_queries(near, wq, cosines, sines)
    wo_other = shift(wo, "c", 1)
    acc_near, state_near = attend_prompt(q_near, cache, prompts[:5])
    far[0] = after(far[0], pairs_near, acc_near)
    pairs_far = project_pairs(far, core_word, wkv, key_cosines, key_sines)
    pairs = jnp.concatenate([pairs_near, pairs_far], axis=0)
    straight = [(g, 2 * g) for g in range(4)] + [(4 + g, 2 * g + 1) for g in range(4)]
    crossed = [(g, 2 * g + 1) for g in range(4)] + [(4 + g, 2 * g) for g in range(4)]
    first, second = lax.ppermute(pairs, chips, straight), lax.ppermute(pairs, chips, crossed)
    far[0] = after(far[0], pairs_far)
    q_far = project_queries(far, wq, cosines, sines)
    wo = merge_rows(after(wo, q_far), wo_other)
    pairs = jnp.stack([after(first, wo), second])
    pairs_other = shift(pairs, "c", 1)
    acc, state = attend_prompt(q_far, cache, prompts[5:])
    pairs_other = after(pairs_other, acc)
    att_far = attend_own(q_far, acc, state, pairs, pairs_other, info[:, 5:])

    p13, p11, p12b, p12a = project_out(att_far, wo, (1, 1, 2))
    across_a = shift(p12a, "xh", 1)
    up = shift(p11, "y", 1)
    down = shift(p13, "y", -1)
    across_b = shift(p12b, "xh", 1)
    att_near = attend_own(
        q_near, acc_near, state_near, after(pairs, p11), pairs_other, info[:, :5]
    )
    p00, p10, p03b, p03a, p01b, p01a, p02b, p02a = project_out(att_near, wo, (1, 1, 2, 2, 2))
    up_a, down_a = split_sum(p02a, across_a)
    across = add(after(p10, up_a), up, down)
    up_b, down_b = split_sum(after(p02b, across), across_b)
    p01a = after(p01a, up_b)
    up_a, down_a = shift(up_a, "y", 1), shift(down_a, "y", -1)
    across = shift(across, "xh", 1)
    up_b, down_b = shift(up_b, "y", 1), shift(down_b, "y", -1)
    p01a, p03a = relay_sum(p01a, up_a, p03a, down_a)
    up_a, down_a = shift(p01a, "y", 1), shift(p03a, "y", -1)
    p01b, p03b = relay_sum(after(p01b, p01a), up_b, p03b, down_b)
    up_b, down_b = shift(p01b, "y", 1), shift(p03b, "y", -1)
    onward = [(i, (i + 1) % 16) for i in range(16)]
    total_a = add(hidden, p00, across, up_a, down_a, start=D // 2)
    total_b = add(after(hidden, total_a), p00, across, up_b, down_b)
    out_a = lax.ppermute(total_a, ("xl", "z"), onward)
    out_b = lax.ppermute(total_b, ("xl", "z"), onward)
    whole = place(out_a, D // 2)
    return place(out_b, 0, whole)


def solution(mesh):
    whole = Mesh(mesh.devices.reshape(2, 8, 2, 4, 2), ("xl", "z", "xh", "y", "c"))
    section, tp = ("xl", "z"), ("xh", "y", "c")
    in_specs = (
        P(section + tp, None),
        P(section, None),
        P(section, None, tp),
        P(section, None, tp),
        P(section, tp, None),
        P(section, None, tp, None),
        P(section),
        P(section),
    )
    out_specs = P(section + tp, None)
    return jax.shard_map(body, mesh=whole, in_specs=in_specs, out_specs=out_specs, check_vma=False)
```

```python
import functools

import jax
import jax.numpy as jnp
from jax import lax
from jax.experimental import pallas as pl
from jax.experimental.pallas import tpu as pltpu
from jax.sharding import Mesh, PartitionSpec as P

D = 8192
QH = 32
KVH = 4
HD = 128
PROMPT = 1024
NPROMPT = 4
RESP = 128
ROWS = 64
EPS = 1e-06
F32 = jnp.float32
BF16 = jnp.bfloat16
VMEM = 12 * 1024 * 1024
BRIEF = pl.CostEstimate(flops=1, bytes_accessed=1, transcendentals=0)

PLACES = ((0, 0), (1, 0), (0, 3), (0, 1), (0, 2), (1, 3), (1, 1), (1, 2))


def shift(value, axis, by):
    size = lax.axis_size(axis)
    return lax.ppermute(value, axis, [(i, (i + by) % size) for i in range(size)])


def params(**kw):
    return pltpu.CompilerParams(vmem_limit_bytes=VMEM, **kw)


def norm_kernel(x_ref, gain_ref, out_ref):
    wide = x_ref[...].astype(F32)
    mean = jnp.mean(wide * wide, axis=-1, keepdims=True)
    out_ref[...] = (wide * lax.rsqrt(mean + EPS) * gain_ref[...]).astype(BF16)


def norm(hidden, gain):
    return pl.pallas_call(
        norm_kernel,
        out_shape=jax.ShapeDtypeStruct((ROWS, D), BF16),
        grid=(2,),
        in_specs=[
            pl.BlockSpec((ROWS // 2, D), lambda i: (i, 0)),
            pl.BlockSpec((1, D), lambda i: (0, 0)),
        ],
        out_specs=pl.BlockSpec((ROWS // 2, D), lambda i: (i, 0)),
        compiler_params=params(),
        cost_estimate=BRIEF,
        name="norm",
    )(hidden, gain)


def turned(value, cosines, sines):
    return value * cosines + pltpu.roll(value, HD // 2, 1) * sines


def merge_kernel(places, *refs):
    out_ref, sems = refs[-2:]
    copies = [
        pltpu.make_async_copy(refs[source].at[there], out_ref.at[here], sems.at[i])
        for i, (source, there, here) in enumerate(places)
    ]
    for copy in copies:
        copy.start()
    for copy in copies:
        copy.wait()


def merge(own, other, shape, places):
    hbm = pl.BlockSpec(memory_space=pl.ANY)
    return pl.pallas_call(
        functools.partial(merge_kernel, places),
        out_shape=jax.ShapeDtypeStruct(shape, BF16),
        in_specs=[hbm, hbm],
        out_specs=pl.BlockSpec(memory_space=pltpu.VMEM),
        scratch_shapes=[pltpu.SemaphoreType.DMA((len(places),))],
        compiler_params=params(),
        cost_estimate=BRIEF,
        name="merge",
    )(own, other)


def merge_columns(own, other):
    rows, cols = own.shape
    every = slice(None)
    places = [
        (i, (every, every), (every, slice(i * cols, (i + 1) * cols))) for i in range(2)
    ]
    return merge(own, other, (rows, 2 * cols), places)


def merge_rows(own, other):
    rows, cols = own.shape
    every = slice(None)
    places = [
        (i, (every, every), (slice(i * rows, (i + 1) * rows), every)) for i in range(2)
    ]
    return merge(own, other, (2 * rows, cols), places)


def merge_cache(own, other):
    every = slice(None)
    places = [
        (i, (every, p), (p, slice(8 * i, 8 * (i + 1)))) for i in range(2) for p in range(NPROMPT)
    ]
    return merge(own, other, (NPROMPT, 16, ROWS, 2 * HD), places)


def query_kernel(count, *refs):
    pieces = refs[:count]
    w_ref, cos_ref, sin_ref, out_ref = refs[count:]
    depth = D // 2
    total = None
    for step in range(2):
        part = slice(step * depth, (step + 1) * depth)
        rows = jnp.concatenate([piece[:, part] for piece in pieces], axis=0)
        term = jnp.dot(rows, w_ref[part, :], preferred_element_type=F32)
        total = term if total is None else total + term
    for block in range(out_ref.shape[0]):
        for head in range(4):
            part = total[block * ROWS : (block + 1) * ROWS, head * HD : (head + 1) * HD]
            out_ref[block, head * ROWS : (head + 1) * ROWS, :] = turned(
                part, cos_ref[...], sin_ref[...]
            ).astype(BF16)


def project_queries(pieces, weight, cosines, sines):
    rows = sum(piece.shape[0] for piece in pieces)
    return pl.pallas_call(
        functools.partial(query_kernel, len(pieces)),
        out_shape=jax.ShapeDtypeStruct((rows // ROWS, 4 * ROWS, HD), BF16),
        compiler_params=params(),
        cost_estimate=BRIEF,
        name="queries",
    )(*pieces, weight, cosines, sines)


def dot_t(a, b):
    return lax.dot_general(a, b, (((1,), (1,)), ((), ())), preferred_element_type=F32)


def pair_kernel(count, *refs):
    pieces = refs[:count]
    core_ref, w_ref, cos_ref, sin_ref, out_ref = refs[count:]
    depth = D // 2
    total = None
    for step in range(2):
        part = slice(step * depth, (step + 1) * depth)
        rows = jnp.concatenate([piece[:, part] for piece in pieces], axis=0)
        term = dot_t(rows, w_ref[:, part])
        total = term if total is None else total + term
    pairs = total.astype(BF16).astype(F32)
    pairs = jnp.where(core_ref[0] == 0, pairs, pltpu.roll(pairs, HD // 2, 1))
    for block in range(out_ref.shape[0]):
        part = pairs[block * ROWS : (block + 1) * ROWS, :]
        out_ref[block] = turned(part, cos_ref[...], sin_ref[...]).astype(BF16)


def project_pairs(pieces, core, weight, cosines, sines):
    rows = sum(piece.shape[0] for piece in pieces)
    vmem = pl.BlockSpec(memory_space=pltpu.VMEM)
    return pl.pallas_call(
        functools.partial(pair_kernel, len(pieces)),
        out_shape=jax.ShapeDtypeStruct((rows // ROWS, ROWS, HD), BF16),
        in_specs=[vmem] * len(pieces) + [pl.BlockSpec(memory_space=pltpu.SMEM)] + [vmem] * 3,
        compiler_params=params(),
        cost_estimate=BRIEF,
        name="pairs",
    )(*pieces, core, weight, cosines, sines)


def sort_kernel(key_ref, value_ref, out_ref):
    out_ref[0, :, :, :HD] = key_ref[...]
    out_ref[0, :, :, HD:] = value_ref[...]


def sort_cache(cache):
    return pl.pallas_call(
        sort_kernel,
        out_shape=jax.ShapeDtypeStruct((2 * KVH, NPROMPT, ROWS, 2 * HD), BF16),
        grid=(2 * KVH,),
        in_specs=[
            pl.BlockSpec((NPROMPT, ROWS, HD), lambda i: (0, 0, i // 2)),
            pl.BlockSpec((NPROMPT, ROWS, HD), lambda i: (0, 0, KVH + i // 2)),
        ],
        out_specs=pl.BlockSpec((1, NPROMPT, ROWS, 2 * HD), lambda i: (i, 0, 0, 0)),
        compiler_params=params(),
        cost_estimate=BRIEF,
        name="sort_cache",
    )(cache, cache)


def prompt_kernel(prompt_ref, q_ref, cache_ref, acc_ref, state_ref):
    lane = lax.broadcasted_iota(jnp.int32, (4 * ROWS, HD), 1)

    @pl.loop(0, q_ref.shape[0])
    def _(i):
        cache = cache_ref[prompt_ref[i]].reshape(PROMPT, 2 * HD)
        scores = dot_t(q_ref[i], cache[:, :HD]) * HD ** (-0.5)
        top = jnp.max(scores, axis=-1, keepdims=True)
        probs = jnp.exp(scores - top)
        total = jnp.sum(probs, axis=-1, keepdims=True)
        acc_ref[i] = jnp.dot(probs.astype(BF16), cache[:, HD:], preferred_element_type=F32)
        state_ref[i] = jnp.where(lane < HD // 2, top, total)


def attend_prompt(queries, cache, prompts):
    shape = jax.ShapeDtypeStruct(queries.shape, F32)
    vmem = pl.BlockSpec(memory_space=pltpu.VMEM)
    return pl.pallas_call(
        prompt_kernel,
        out_shape=(shape, shape),
        in_specs=[pl.BlockSpec(memory_space=pltpu.SMEM), vmem, vmem],
        compiler_params=params(),
        cost_estimate=BRIEF,
        name="attend_prompt",
    )(prompts, queries, cache)


def own_kernel(info_ref, q_ref, acc_ref, state_ref, own_ref, other_ref, out_ref):
    lane = lax.broadcasted_iota(jnp.int32, (4 * ROWS, HD), 1)
    line = lax.broadcasted_iota(jnp.int32, (4 * ROWS, HD), 0) % ROWS

    @pl.loop(0, q_ref.shape[0])
    def _(i):
        length, core, kind = info_ref[0, i], info_ref[1, i], info_ref[2, i]
        key_at, value_at = info_ref[3, i], info_ref[4, i]
        keys = jnp.concatenate([own_ref[kind, key_at], other_ref[kind, key_at]], axis=0)
        values = jnp.concatenate(
            [own_ref[1 - kind, value_at], other_ref[1 - kind, value_at]], axis=0
        )
        scores = dot_t(q_ref[i], keys) * HD ** (-0.5)
        row = line + core * ROWS
        place = jnp.where(lane < ROWS, lane + core * ROWS, lane - core * ROWS)
        visible = (place <= row) & (place < length)
        scores = jnp.where(visible, scores, -jnp.inf)
        state = state_ref[i]
        top_a = state[:, :1]
        total_a = state[:, HD // 2 : HD // 2 + 1]
        top = jnp.maximum(top_a, jnp.max(scores, axis=-1, keepdims=True))
        scale = jnp.exp(top_a - top)
        probs = jnp.exp(scores - top)
        total = total_a * scale + jnp.sum(probs, axis=-1, keepdims=True)
        blended = acc_ref[i] * scale + jnp.dot(
            probs.astype(BF16), values, preferred_element_type=F32
        )
        blended = jnp.where(row < length, blended / total, 0.0).astype(BF16)
        for head in range(4):
            out_ref[i, :, head * HD : (head + 1) * HD] = blended[
                head * ROWS : (head + 1) * ROWS, :
            ]


def attend_own(queries, acc, state, pairs_own, pairs_other, info):
    count = queries.shape[0]
    vmem = pl.BlockSpec(memory_space=pltpu.VMEM)
    out = pl.pallas_call(
        own_kernel,
        out_shape=jax.ShapeDtypeStruct((count, ROWS, 4 * HD), BF16),
        in_specs=[pl.BlockSpec(memory_space=pltpu.SMEM)] + [vmem] * 5,
        compiler_params=params(),
        cost_estimate=BRIEF,
        name="attend_own",
    )(info, queries, acc, state, pairs_own, pairs_other)
    return out.reshape(count * ROWS, 4 * HD)


def output_kernel(counts, x_ref, w_ref, *out_refs):
    tile = 1024

    @pl.loop(0, D // 2 // tile)
    def _(step):
        inner = pl.ds(pl.multiple_of(step * tile, tile), tile)
        for side in range(2):
            part = pl.ds(pl.multiple_of(side * (D // 2) + step * tile, tile), tile)
            total = jnp.dot(x_ref[...], w_ref[:, part], preferred_element_type=F32)
            total = total.astype(BF16)
            at = 0
            for block, count in enumerate(counts):
                rows = total[block * ROWS : (block + 1) * ROWS, :]
                if count == 1:
                    out_refs[at][:, part] = rows
                else:
                    out_refs[at + side][:, inner] = rows
                at += count


def project_out(attended, weight, counts):
    return pl.pallas_call(
        functools.partial(output_kernel, counts),
        out_shape=[
            jax.ShapeDtypeStruct((ROWS, D // count), BF16) for count in counts for _ in range(count)
        ],
        compiler_params=params(),
        cost_estimate=BRIEF,
        name="project_out",
    )(attended, weight)


def sum_kernel(start, *refs):
    width = refs[-1].shape[1]
    total = 0.0
    for ref in refs[:-1]:
        low = start if ref.shape[1] > width else 0
        total += ref[:, low : low + width].astype(F32)
    refs[-1][...] = total.astype(BF16)


def split_kernel(a_ref, b_ref, low_ref, high_ref):
    total = (a_ref[...].astype(F32) + b_ref[...].astype(F32)).astype(BF16)
    half = low_ref.shape[1]
    low_ref[...] = total[:, :half]
    high_ref[...] = total[:, half:]


def split_sum(a, b):
    half = jax.ShapeDtypeStruct((a.shape[0], a.shape[1] // 2), BF16)
    return pl.pallas_call(
        split_kernel,
        out_shape=(half, half),
        compiler_params=params(),
        cost_estimate=BRIEF,
        name="split_sum",
    )(a, b)


def place_kernel(start, *refs):
    value_ref, out_ref, sem = refs[-3:]
    width = value_ref.shape[1]
    copy = pltpu.make_async_copy(value_ref, out_ref.at[:, pl.ds(start, width)], sem)
    copy.start()
    copy.wait()


def place(value, start, whole=None):
    hbm = pl.BlockSpec(memory_space=pl.ANY)
    given = () if whole is None else (whole,)
    return pl.pallas_call(
        functools.partial(place_kernel, start),
        out_shape=jax.ShapeDtypeStruct((ROWS, D), BF16),
        in_specs=[hbm] * (len(given) + 1),
        out_specs=hbm,
        scratch_shapes=[pltpu.SemaphoreType.DMA],
        input_output_aliases={0: 0} if given else {},
        compiler_params=params(),
        cost_estimate=BRIEF,
        name="place",
    )(*given, value)


def relay_kernel(a_ref, up_ref, b_ref, down_ref, a_out, b_out):
    half = up_ref.shape[1]
    a_out[:, :half] = (a_ref[:, :half].astype(F32) + up_ref[...].astype(F32)).astype(BF16)
    a_out[:, half:] = a_ref[:, half:]
    b_out[:, :half] = b_ref[:, :half]
    b_out[:, half:] = (b_ref[:, half:].astype(F32) + down_ref[...].astype(F32)).astype(BF16)


def relay_sum(a, up, b, down):
    whole = jax.ShapeDtypeStruct(a.shape, BF16)
    return pl.pallas_call(
        relay_kernel,
        out_shape=(whole, whole),
        compiler_params=params(),
        cost_estimate=BRIEF,
        name="relay_sum",
    )(a, up, b, down)


def add(*terms, start=0):
    width = min(term.shape[1] for term in terms)
    return pl.pallas_call(
        functools.partial(sum_kernel, start),
        out_shape=jax.ShapeDtypeStruct((terms[0].shape[0], width), BF16),
        compiler_params=params(),
        cost_estimate=BRIEF,
        name="add",
    )(*terms)


def after(value, *others):
    return lax.optimization_barrier((value, *others))[0]


def rope_tables():
    half = HD // 2
    position = (PROMPT + jnp.arange(RESP)).astype(F32)
    inverse = jnp.exp(-(2.0 * jnp.arange(half).astype(F32) / HD) * jnp.log(10000.0))
    angles = position[:, None] * inverse[None, :]
    cosines, sines = jnp.cos(angles), jnp.sin(angles)
    return (
        jnp.concatenate([cosines, cosines], axis=1),
        jnp.concatenate([-sines, sines], axis=1),
    )


def body(hidden, norm_gain, query_weight, kv_weight, out_weight, prompt_cache, resp_len, prompt_id):
    xh, y, core = lax.axis_index("xh"), lax.axis_index("y"), lax.axis_index("c")
    wq, wkv, wo = query_weight[0], kv_weight[0].T, out_weight[0]
    chips = ("xh", "y")

    normed = norm(hidden, norm_gain)
    b10 = shift(normed, "xh", 1)
    b03 = shift(normed, "y", 1)
    b01 = shift(normed, "y", -1)
    wkv_other = shift(wkv, "c", 1)
    wq_other = shift(wq, "c", 1)
    cache = sort_cache(after(prompt_cache[0], normed))
    cache = lax.all_to_all(cache, chips, 0, 0, tiled=True)

    cosines, sines = rope_tables()
    cosines = lax.dynamic_slice_in_dim(cosines, core * ROWS, ROWS, 0)
    sines = lax.dynamic_slice_in_dim(sines, core * ROWS, ROWS, 0)
    key_cosines = jnp.where(xh == 0, cosines, 1.0)
    key_sines = jnp.where(xh == 0, sines, 0.0)

    def pick(values, index):
        lanes = jnp.arange(8)
        return jnp.sum(jnp.where(index[:, None] == lanes[None, :], values[None, :], 0), axis=1)

    responses = jnp.stack([(xh ^ dx) * 4 + (y + dy) % 4 for dx, dy in PLACES])
    prompts = pick(prompt_id, responses).astype(jnp.int32)
    lengths = pick(resp_len, responses)
    maker_y = xh * 2 + y // 2
    table = [0] * 8
    for at, (dx, dy) in enumerate(PLACES):
        table[dx * 4 + dy] = at
    table = jnp.array(table, jnp.int32)
    away = (responses % 4 - maker_y) % 4
    key_at = pick(table, (responses // 4) * 4 + away)
    value_at = pick(table, (1 - responses // 4) * 4 + away)
    info = jnp.stack(
        [
            lengths,
            jnp.full((8,), core, jnp.int32),
            jnp.full((8,), y % 2, jnp.int32),
            key_at,
            value_at,
        ]
    ).astype(jnp.int32)
    core_word = jnp.full((1,), core, jnp.int32)

    b03 = after(b03, b10, wq_other, wkv_other, info, prompts, key_cosines, key_sines, core_word)
    b01 = after(b01, b03, cache)
    upper, lower = b03[: ROWS // 2], b01[ROWS // 2 :]
    top02 = shift(upper, "y", 1)
    low02 = shift(lower, "y", -1)
    wkv = merge_rows(after(wkv, lower), wkv_other)
    wq = merge_columns(after(wq, lower), wq_other)
    b02 = jnp.concatenate([after(top02, wkv, wq), low02], axis=0)
    b12 = shift(b02, "xh", 1)
    b10 = after(b10, lower)
    b13 = shift(b10, "y", 1)
    b11 = shift(b10, "y", -1)
    cache = after(cache, lower)
    cache = merge_cache(cache, shift(cache, "c", 1))

    near = [normed, b10, b03, b01, b02]
    far = [b13, b11, b12]
    pairs_near = project_pairs(near, core_word, wkv, key_cosines, key_sines)
    q_near = project_queries(near, wq, cosines, sines)
    wo_other = shift(wo, "c", 1)
    acc_near, state_near = attend_prompt(q_near, cache, prompts[:5])
    far[0] = after(far[0], pairs_near, acc_near)
    pairs_far = project_pairs(far, core_word, wkv, key_cosines, key_sines)
    pairs = jnp.concatenate([pairs_near, pairs_far], axis=0)
    straight = [(g, 2 * g) for g in range(4)] + [(4 + g, 2 * g + 1) for g in range(4)]
    crossed = [(g, 2 * g + 1) for g in range(4)] + [(4 + g, 2 * g) for g in range(4)]
    first, second = lax.ppermute(pairs, chips, straight), lax.ppermute(pairs, chips, crossed)
    far[0] = after(far[0], pairs_far)
    q_far = project_queries(far, wq, cosines, sines)
    wo = merge_rows(after(wo, q_far), wo_other)
    pairs = jnp.stack([after(first, wo), second])
    pairs_other = shift(pairs, "c", 1)
    acc, state = attend_prompt(q_far, cache, prompts[5:])
    pairs_other = after(pairs_other, acc)
    att_far = attend_own(q_far, acc, state, pairs, pairs_other, info[:, 5:])

    p13b, p13a, p11b, p11a, p12b, p12a = project_out(att_far, wo, (2, 2, 2))
    across_a = shift(p12a, "xh", 1)
    up_a, down_a = shift(p11a, "y", 1), shift(p13a, "y", -1)
    across_b = shift(p12b, "xh", 1)
    att_near = attend_own(
        q_near, acc_near, state_near, after(pairs, p11a), pairs_other, info[:, :5]
    )
    p00, p10b, p10a, p03b, p03a, p01b, p01a, p02b, p02a = project_out(
        att_near, wo, (1, 2, 2, 2, 2)
    )
    p11b = after(p11b, p00)
    from_b, onto_b = shift(p11b, "y", 1), shift(after(p13b, p00), "y", -1)
    from_a, onto_a = up_a, down_a
    up_a, down_a = split_sum(p02a, across_a)
    up_b, down_b = split_sum(after(p02b, up_a), across_b)
    over_a = add(after(p10a, up_a), from_a, onto_a)
    over_b = add(after(p10b, over_a), from_b, onto_b)
    up_a, down_a = shift(up_a, "y", 1), shift(down_a, "y", -1)
    up_b, down_b = shift(up_b, "y", 1), shift(down_b, "y", -1)
    over_a, over_b = shift(over_a, "xh", 1), shift(over_b, "xh", 1)
    p01a, p03a = relay_sum(p01a, up_a, p03a, down_a)
    up_a, down_a = shift(p01a, "y", 1), shift(p03a, "y", -1)
    p01b, p03b = relay_sum(after(p01b, p01a), up_b, p03b, down_b)
    up_b, down_b = shift(p01b, "y", 1), shift(p03b, "y", -1)
    onward = [(i, (i + 1) % 16) for i in range(16)]
    total_a = add(hidden, p00, over_a, up_a, down_a, start=D // 2)
    total_b = add(after(hidden, total_a), p00, over_b, up_b, down_b)
    out_a = lax.ppermute(total_a, ("xl", "z"), onward)
    out_b = lax.ppermute(total_b, ("xl", "z"), onward)
    whole = place(out_a, D // 2)
    return place(out_b, 0, whole)


def solution(mesh):
    whole = Mesh(mesh.devices.reshape(2, 8, 2, 4, 2), ("xl", "z", "xh", "y", "c"))
    section, tp = ("xl", "z"), ("xh", "y", "c")
    in_specs = (
        P(section + tp, None),
        P(section, None),
        P(section, None, tp),
        P(section, None, tp),
        P(section, tp, None),
        P(section, None, tp, None),
        P(section),
        P(section),
    )
    out_specs = P(section + tp, None)
    return jax.shard_map(body, mesh=whole, in_specs=in_specs, out_specs=out_specs, check_vma=False)
```
